32 devices in a mesh: slab: 2 (over y), frames: 4 (over z), medoids: 4 (over x, core).
Axes of the slice: x: 2, y: 2, z: 4, core: 2. Of those that a mesh axis runs over, the one named last changes fastest.
Arguments:
- frames: bfloat16 [16384, 512], P(('slab', 'frames')), parts along dimension 0, may hold values from -6 to 6
- medoids: bfloat16 [4, 8192, 512], P('medoids', 'frames'), may hold values from -6 to 6
- tile_ids: int32 [4, 128, 24], P('medoids', ('slab', 'frames')), parts along dimension 1, may hold values from 0 to 63, as said below
- tile_counts: int32 [4, 128], P('medoids', ('slab', 'frames')), parts along dimension 1, may hold values from 1 to 24, as said below
- plan: int32 [128], P('slab'), parts along dimension 0, may hold values from 0 to 63, as said below
Outputs:
- nearest: float32 [16384], P(('slab', 'frames')), parts along dimension 0
- second: float32 [16384], P(('slab', 'frames')), parts along dimension 0
The draws below stay inside these ranges and needn't reach their ends.
There are 2 independent parts, one for each index of `slab`. The reference program is written for one: setup_inputs(seed, part) draws one part's arguments, and reference() takes and returns one part's arrays. A program takes and returns all parts, laid end to end along the dimension named above; an argument that names none is the same for every part. Nothing has to cross between parts.
Inputs may be any that keep to these rules, and one draw needn't show every extreme that they name: plan is a permutation. Of the frame tiles 16 i to 16 i + 15, at most 4 stand at positions 16 j to 16 j + 15 of plan's inverse for one j, and exactly 4 for some j, for every i. `tile_ids`: the 24 entries of one list are distinct; entries at l >= tile_counts[m, g] are ignored. `tile_counts`: the largest value is reached in every draw.
All inputs are finite; a program needn't handle non-finite values.
Results may differ from the reference program's by a relative error of at most 0.0003.
Values may be sent and summed in bfloat16 or wider, within the bound.
A program may use at most 64 MiB of HBM per device.

```python
import jax
import jax.numpy as jnp
from jax import lax

D = 512
MEDOIDS = 32768
TILE = 128
LMAX = 24
B_DEV = 16
GROUPS = 4
GROUP_SIZE = 8192
GROUP_TILES = 64
TILES = 64
FRAMES = 8192


def draw_tile_ids(key, part):
    group_tiles = MEDOIDS // (GROUPS * TILE)
    base = jax.random.fold_in(key, 11)
    keys = jax.random.split(base, GROUPS * TILES)
    lists = jax.vmap(lambda one: jax.random.permutation(one, group_tiles)[:LMAX])(keys)
    return lists.reshape(GROUPS, TILES, LMAX).astype(jnp.int32)


def draw_tile_counts(key, part):
    base = jax.random.fold_in(key, 23)
    first_key, second_key, third_key = jax.random.split(base, 3)
    members = TILES // B_DEV
    level = jax.random.randint(first_key, (members,), 0, 4)
    upper = LMAX // 8 * jnp.left_shift(jnp.ones_like(level), level)
    upper = jnp.repeat(upper, B_DEV)
    counts = jax.random.randint(second_key, (GROUPS, TILES), 1, upper[None, :] + 1)
    forced = jax.random.randint(third_key, (), 0, TILES)
    counts = counts.at[:, forced].set(LMAX)
    return counts.astype(jnp.int32)


def draw_plan(key, part):
    base = jax.random.fold_in(key, 37)
    first_key, second_key, third_key, fourth_key = jax.random.split(base, 4)
    members = TILES // B_DEV
    shuffled = jax.random.permutation(first_key, members)
    entries = jnp.arange(B_DEV)
    picks = entries % members
    shifts = shuffled[picks]
    relabel = jax.random.permutation(second_key, members)
    relabel_inverse = jnp.zeros((members,), jnp.int32).at[relabel].set(jnp.arange(members, dtype=jnp.int32))
    target_perm = jax.vmap(lambda one: jax.random.permutation(one, B_DEV))(jax.random.split(third_key, members))
    source_perm = jax.vmap(lambda one: jax.random.permutation(one, B_DEV))(jax.random.split(fourth_key, members))
    target = jnp.arange(members)[:, None]
    entry = entries[None, :]
    source = (relabel_inverse[target] - shifts[entry]) % members
    source_tile = source * B_DEV + source_perm[source, entry]
    position = target * B_DEV + target_perm[target, entry]
    plan = jnp.zeros((TILES,), jnp.int32).at[position.reshape(-1)].set(source_tile.reshape(-1).astype(jnp.int32))
    return plan


def levels(stream_key, shape, cuts, least, high):
    level, own = 1.0, jax.random.fold_in(stream_key, 6)
    for axis_at, shards_of in cuts:
        heights = jnp.exp(jax.random.uniform(jax.random.fold_in(own, axis_at), (shards_of,), jnp.float32, least / len(cuts), high / len(cuts)))
        level = level * jnp.repeat(heights, shape[axis_at] // shards_of).reshape([-1 if axis == axis_at else 1 for axis in range(len(shape))])
    return level


def scatter_about(rng, dims, deviation, limit, cuts=(), held_as=jnp.bfloat16):
    array = jax.random.normal(rng, dims, jnp.float32) * deviation
    if len(cuts) > 0:
        array = levels(rng, dims, cuts, -0.22, 0.18) * array
    return jnp.clip(array, min=-limit, max=limit).astype(held_as)


def setup_inputs(seed: int = 0, part: int = 0) -> dict:
    arg_keys = jax.random.split(jax.random.key(seed), 6)
    own_keys = jax.random.split(jax.random.fold_in(arg_keys[5], part), 6)
    return {
        "frames": scatter_about(own_keys[0], (FRAMES, D), 1.0, 6.0, ((0, 4),)),
        "medoids": scatter_about(arg_keys[1], (GROUPS, GROUP_SIZE, D), 1.0, 6.0, ((0, 4), (1, 4))),
        "tile_ids": draw_tile_ids(jax.random.fold_in(jax.random.fold_in(arg_keys[5], part), 71), part),
        "tile_counts": draw_tile_counts(jax.random.fold_in(jax.random.fold_in(arg_keys[5], part), 71), part),
        "plan": draw_plan(jax.random.fold_in(jax.random.fold_in(arg_keys[5], part), 71), part),
    }


big_value = 1e30
per_block = 8


def fold_two(left_one, left_two, right_one, right_two):
    first = jnp.minimum(left_one, right_one)
    second = jnp.minimum(jnp.maximum(left_one, right_one), jnp.minimum(left_two, right_two))
    return first, second


def tile_pass(frame_tile, ids, count, group_rows, group_norm):
    width = frame_tile.shape[1]
    rows_tile = frame_tile.shape[0]
    frame_norm = jnp.sum(jnp.square(frame_tile.astype(jnp.float32)), axis=1)

    def step(block, carry):
        start = (block * per_block).astype(jnp.int32)
        chosen = lax.dynamic_slice_in_dim(ids, start, per_block)
        live = (start + jnp.arange(per_block, dtype=jnp.int32)) < count
        rows = group_rows[chosen].reshape(per_block * rows_tile, width)
        norms = group_norm[chosen].reshape(per_block * rows_tile)
        inner = lax.dot_general(frame_tile, rows, (((1,), (1,)), ((), ())), preferred_element_type=jnp.float32)
        dist = (frame_norm[:, None] + norms[None, :] - 2.0 * inner) / width
        keep = jnp.repeat(live, rows_tile)
        dist = jnp.where(keep[None, :], dist, jnp.float32(big_value))
        lowest = -lax.top_k(-dist, 2)[0]
        return fold_two(carry[0], carry[1], lowest[:, 0], lowest[:, 1])

    start_pair = (jnp.full((rows_tile,), big_value, jnp.float32), jnp.full((rows_tile,), big_value, jnp.float32))
    blocks = (count + per_block - 1) // per_block
    return lax.fori_loop(0, blocks, step, start_pair)


def reference(frames, medoids, tile_ids, tile_counts, plan):
    tiles = frames.reshape(TILES, TILE, D)
    rows = medoids.reshape(GROUPS, GROUP_TILES, TILE, D)
    norms = jnp.sum(jnp.square(medoids.astype(jnp.float32)), axis=2).reshape(GROUPS, GROUP_TILES, TILE)

    def one_tile(index):
        best_one = jnp.full((TILE,), big_value, jnp.float32)
        best_two = jnp.full((TILE,), big_value, jnp.float32)
        for group in range(GROUPS):
            found_one, found_two = tile_pass(tiles[index], tile_ids[group, index], tile_counts[group, index], rows[group], norms[group])
            best_one, best_two = fold_two(best_one, best_two, found_one, found_two)
        return best_one, best_two

    first, second_all = lax.map(one_tile, jnp.arange(TILES, dtype=jnp.int32))
    return first[plan].reshape(FRAMES), second_all[plan].reshape(FRAMES)
```

```python
import functools

import jax
import jax.numpy as jnp
from jax import lax
from jax.experimental import pallas as pl
from jax.experimental.pallas import tpu as pltpu
from jax.sharding import PartitionSpec as P

TILE = 128
BIG = 1e30
UNROLL = 4
LANES = 128
MESH = pl.DeviceIdType.MESH
F32 = jnp.float32


def remote(src, dst, send, recv, where):
    return pltpu.make_async_remote_copy(
        src_ref=src, dst_ref=dst, send_sem=send, recv_sem=recv, device_id=where, device_id_type=MESH
    )


def greet(targets):
    barrier = pltpu.get_barrier_semaphore()
    for where in targets:
        pl.semaphore_signal(barrier, inc=1, device_id=where, device_id_type=MESH)
    pl.semaphore_wait(barrier, len(targets))


def frame_gather_kernel(
    members, copies, parts, frames, meta, norm, all_frames, all_meta, all_norm,
    own_sem, meta_send, meta_recv, norm_send, norm_recv,
    right_send, left_send, chain_recv, swap_send, swap_recv,
):
    me = lax.axis_index("frames")
    rep = lax.axis_index("medoids")
    blocks = frames.shape[0]
    share = blocks // copies
    piece = share // parts
    levels = copies.bit_length() - 1

    partners = []
    for level in range(levels):
        bit = copies >> (level + 1)
        partners.append((bit, {"medoids": rep + bit - 2 * bit * lax.rem(rep // bit, 2)}))
    others = [{"frames": lax.rem(me + k, members)} for k in range(1, members)]
    greet(others + [p[1] for p in partners])

    def place(block, owner_rep, part):
        return pl.ds(block * blocks + owner_rep * share + part * piece, piece)

    def chain(block, part, src, sends, to):
        return remote(
            src, all_frames.at[place(block, rep, part)], sends.at[block, part],
            chain_recv.at[block, part], {"frames": to},
        )

    def own_part(part):
        return frames.at[pl.ds(rep * share + part * piece, piece)]

    def held_part(block, part):
        return all_frames.at[place(block, rep, part)]

    for part in range(parts):
        @pl.when(me < members - 1)
        def _():
            chain(me, part, own_part(part), right_send, me + 1).start()

        @pl.when(me > 0)
        def _():
            chain(me, part, own_part(part), left_send, me - 1).start()

    own = pltpu.make_async_copy(frames, all_frames.at[pl.ds(me * blocks, blocks)], own_sem.at[0])
    own.start()
    own_meta = pltpu.make_async_copy(meta, all_meta.at[me], own_sem.at[1])
    own_meta.start()
    own_norm = pltpu.make_async_copy(norm, all_norm.at[me], own_sem.at[2])
    own_norm.start()
    small = []
    for k, where in enumerate(others):
        small.append(remote(meta, all_meta.at[me], meta_send.at[k], meta_recv.at[k], where))
        small.append(remote(norm, all_norm.at[me], norm_send.at[k], norm_recv.at[k], where))
    for copy in small:
        copy.start()

    def swap(block, part, level, index):
        holder = rep
        for earlier in range(level):
            if (index >> earlier) & 1:
                bit = partners[earlier][0]
                holder = holder + bit - 2 * bit * lax.rem(rep // bit, 2)
        slot = (1 << level) - 1 + index
        ref = all_frames.at[place(block, holder, part)]
        return remote(
            ref, ref, swap_send.at[block, part, slot], swap_recv.at[block, part, slot],
            partners[level][1],
        )

    def sides(step):
        return ((me - step >= 0, me - step, 0), (me + step <= members - 1, me + step, 1))

    def at_arrival(step, part):
        for exists, block, side in sides(step):
            @pl.when(exists)
            def _():
                chain(block, part, held_part(block, part), right_send, me).wait_recv()
                if side == 0:
                    @pl.when(me < members - 1)
                    def _():
                        chain(block, part, held_part(block, part), right_send, me + 1).start()
                else:
                    @pl.when(me > 0)
                    def _():
                        chain(block, part, held_part(block, part), left_send, me - 1).start()
                for level in range(levels):
                    swap(block, part, level, 0).start()

    def at_level(step, part, level):
        for exists, block, _side in sides(step):
            @pl.when(exists)
            def _():
                for index in range(1 << level):
                    swap(block, part, level, index).wait_recv()
                    mine = index | (1 << level)
                    for later in range(level + 1, levels):
                        swap(block, part, later, mine).start()

    units = [(step, part) for step in range(1, members) for part in range(parts)]
    for turn in range(len(units) + levels):
        if turn < len(units):
            at_arrival(*units[turn])
        for level in range(levels):
            unit = turn - 1 - level
            if 0 <= unit < len(units):
                at_level(*units[unit], level)

    own.wait()
    own_meta.wait()
    own_norm.wait()
    for copy in small:
        copy.wait_send()
        copy.wait_recv()
    for part in range(parts):
        @pl.when(me < members - 1)
        def _():
            chain(me, part, own_part(part), right_send, me + 1).wait_send()

        @pl.when(me > 0)
        def _():
            chain(me, part, own_part(part), left_send, me - 1).wait_send()
    for step, part in units:
        for exists, block, side in sides(step):
            @pl.when(exists)
            def _():
                if side == 0:
                    @pl.when(me < members - 1)
                    def _():
                        chain(block, part, held_part(block, part), right_send, me + 1).wait_send()
                else:
                    @pl.when(me > 0)
                    def _():
                        chain(block, part, held_part(block, part), left_send, me - 1).wait_send()
                for level in range(levels):
                    for index in range(1 << level):
                        swap(block, part, level, index).wait_send()


def gather_frames(mesh, tiles, meta, norm):
    members, copies = mesh.shape["frames"], mesh.shape["medoids"]
    blocks = tiles.shape[0]
    share = blocks // copies
    parts = 2 if share % 2 == 0 else 1
    dma = pltpu.SemaphoreType.DMA
    hbm = pl.BlockSpec(memory_space=pl.ANY)
    slots = max(copies - 1, 1)
    all_tiles, all_meta, all_norm = pl.pallas_call(
        functools.partial(frame_gather_kernel, members, copies, parts),
        out_shape=(
            jax.ShapeDtypeStruct((members * blocks,) + tiles.shape[1:], tiles.dtype),
            jax.ShapeDtypeStruct((members,) + meta.shape, meta.dtype),
            jax.ShapeDtypeStruct((members,) + norm.shape, norm.dtype),
        ),
        in_specs=[hbm] * 3,
        out_specs=(hbm,) * 3,
        scratch_shapes=[
            dma((3,)), dma((members,)), dma((members,)), dma((members,)), dma((members,)),
            dma((members, parts)), dma((members, parts)), dma((members, parts)),
            dma((members, parts, slots)), dma((members, parts, slots)),
        ],
        compiler_params=pltpu.CompilerParams(collective_id=0, has_side_effects=True),
        name="gather_frames",
    )(tiles, meta, norm)
    return all_tiles, all_meta.reshape(-1, LANES), all_norm.reshape(-1, LANES)


def medoid_gather_kernel(members, part, whole, own_sem, send_sem, recv_sem):
    me = lax.axis_index("frames")
    count = part.shape[0]
    others = [{"frames": lax.rem(me + k, members)} for k in range(1, members)]
    if others:
        greet(others)
    mine = whole.at[pl.ds(me * count, count)]
    own = pltpu.make_async_copy(part, mine, own_sem)
    own.start()
    sent = [remote(part, mine, send_sem.at[k], recv_sem.at[k], w) for k, w in enumerate(others)]
    for copy in sent:
        copy.start()
    own.wait()
    for copy in sent:
        copy.wait_send()
        copy.wait_recv()


def gather_medoids(mesh, tiles):
    members = mesh.shape["frames"]
    dma = pltpu.SemaphoreType.DMA
    return pl.pallas_call(
        functools.partial(medoid_gather_kernel, members),
        out_shape=jax.ShapeDtypeStruct((members * tiles.shape[0],) + tiles.shape[1:], tiles.dtype),
        in_specs=[pl.BlockSpec(memory_space=pl.ANY)],
        out_specs=pl.BlockSpec(memory_space=pl.ANY),
        scratch_shapes=[dma, dma((members,)), dma((members,))],
        compiler_params=pltpu.CompilerParams(collective_id=1, has_side_effects=True),
        name="gather_medoids",
    )(tiles)


def fold_two(left_one, left_two, right_one, right_two):
    first = jnp.minimum(left_one, right_one)
    second = jnp.minimum(jnp.maximum(left_one, right_one), jnp.minimum(left_two, right_two))
    return first, second


def pairs_kernel(
    longest, base, meta, plan, frames, norm, medoids, out,
    queue_frame, queue_medoid, half_norm, best_one, best_two, final_one, final_two,
):
    number = frames.shape[0]
    held = medoids.shape[0]
    width = frames.shape[2]
    rows = 8
    medoid_base, frame_base = base[0], base[1]

    def half(index, carry):
        tile = medoids[index].astype(F32)
        total = jnp.sum(tile * tile, axis=1, keepdims=True) * 0.5
        half_norm[index] = jnp.broadcast_to(total, (TILE, TILE))
        return carry

    lax.fori_loop(0, held, half, 0)

    def list_of(index, at):
        def entry(place, at):
            medoid = meta[index, place] - medoid_base
            queue_frame[at] = index
            queue_medoid[at] = medoid
            inside = jnp.logical_and(medoid >= 0, medoid < held)
            return at + inside.astype(jnp.int32)

        return lax.fori_loop(0, meta[index, longest], entry, at)

    length = lax.fori_loop(0, number, list_of, jnp.int32(0))
    for k in range(UNROLL):
        queue_frame[length + k] = number
        queue_medoid[length + k] = 0

    best_one[...] = jnp.full(best_one.shape, BIG, F32)
    best_two[...] = jnp.full(best_two.shape, BIG, F32)

    def work(step, carry):
        found = []
        for k in range(UNROLL):
            at = step * UNROLL + k
            row = queue_frame[at]
            medoid = queue_medoid[at]
            frame = jnp.minimum(row, number - 1)
            inner = lax.dot_general(
                medoids[medoid], frames[frame], (((1,), (1,)), ((), ())),
                preferred_element_type=F32,
            )
            value = half_norm[medoid] - inner
            chains = []
            for start in range(0, TILE, 4 * rows):
                parts = [value[start + i * rows:start + (i + 1) * rows] for i in range(4)]
                a, b = jnp.minimum(parts[0], parts[1]), jnp.maximum(parts[0], parts[1])
                c, d = jnp.minimum(parts[2], parts[3]), jnp.maximum(parts[2], parts[3])
                chains.append(fold_two(a, b, c, d))
            while len(chains) > 1:
                chains = [fold_two(*chains[i], *chains[i + 1]) for i in range(0, len(chains), 2)]
            found.append((row, chains[0]))
        for row, (one, two) in found:
            best_one[row], best_two[row] = fold_two(best_one[row], best_two[row], one, two)
        return carry

    lax.fori_loop(0, (length + UNROLL - 1) // UNROLL, work, 0)

    one, two = best_one[:number, 0, :], best_two[:number, 0, :]
    for i in range(1, rows):
        one, two = fold_two(one, two, best_one[:number, i, :], best_two[:number, i, :])
    final_one[...] = (norm[...] + 2.0 * one) / width
    final_two[...] = (norm[...] + 2.0 * two) / width

    def arrange(position, carry):
        source = plan[position] - frame_base
        mine = jnp.logical_and(source >= 0, source < number)
        row = jnp.clip(source, 0, number - 1)
        out[0, pl.ds(position, 1), :] = jnp.where(mine, final_one[pl.ds(row, 1), :], BIG)
        out[1, pl.ds(position, 1), :] = jnp.where(mine, final_two[pl.ds(row, 1), :], BIG)
        return carry

    lax.fori_loop(0, plan.shape[0], arrange, 0)


def pair_minima(base, meta, plan, tiles, norm, medoid_tiles, longest):
    number, held = tiles.shape[0], medoid_tiles.shape[0]
    smem = pl.BlockSpec(memory_space=pltpu.SMEM)
    vmem = pl.BlockSpec(memory_space=pltpu.VMEM)
    room = number * longest + 2 * UNROLL
    return pl.pallas_call(
        functools.partial(pairs_kernel, longest),
        out_shape=jax.ShapeDtypeStruct((2, plan.shape[0], TILE), F32),
        in_specs=[smem, smem, smem, vmem, vmem, vmem],
        out_specs=vmem,
        scratch_shapes=[
            pltpu.SMEM((room,), jnp.int32),
            pltpu.SMEM((room,), jnp.int32),
            pltpu.VMEM((held, TILE, TILE), F32),
            pltpu.VMEM((number + 1, 8, TILE), F32),
            pltpu.VMEM((number + 1, 8, TILE), F32),
            pltpu.VMEM((number, TILE), F32),
            pltpu.VMEM((number, TILE), F32),
        ],
        compiler_params=pltpu.CompilerParams(vmem_limit_bytes=40 * 1024 * 1024),
        name="pair_minima",
    )(base, meta, plan, tiles, norm, medoid_tiles)


def fold_kernel(
    members, groups, part, first, second, from_members, joined, from_groups,
    send_one, recv_one, send_two, recv_two,
):
    me = lax.axis_index("frames")
    group = lax.axis_index("medoids")
    blocks = first.shape[0]
    ways = [lax.rem(me + k, members) for k in range(1, members)]
    greet(
        [{"frames": w} for w in ways]
        + [{"medoids": lax.rem(group + k, groups)} for k in range(1, groups)]
    )
    copies = []
    for k, way in enumerate(ways):
        rows = pl.ds(pl.multiple_of(way * blocks, blocks), blocks)
        copies.append(
            remote(part.at[:, rows, :], from_members.at[k], send_one.at[k], recv_one.at[k], {"frames": way})
        )
    for copy in copies:
        copy.start()
    mine = pl.ds(pl.multiple_of(me * blocks, blocks), blocks)
    one, two = part[0, mine, :], part[1, mine, :]
    for k, copy in enumerate(copies):
        copy.wait_recv()
        one, two = fold_two(one, two, from_members[k, 0], from_members[k, 1])
    joined[0] = one
    joined[1] = two
    across = []
    for k in range(groups - 1):
        across.append(
            remote(
                joined, from_groups.at[k], send_two.at[k], recv_two.at[k],
                {"medoids": lax.rem(group + k + 1, groups)},
            )
        )
    for copy in across:
        copy.start()
    for k, copy in enumerate(across):
        copy.wait_recv()
        one, two = fold_two(one, two, from_groups[k, 0], from_groups[k, 1])
    first[...] = one
    second[...] = two
    for copy in copies + across:
        copy.wait_send()


def fold_everywhere(mesh, part, blocks):
    members, groups = mesh.shape["frames"], mesh.shape["medoids"]
    dma = pltpu.SemaphoreType.DMA
    vmem = pl.BlockSpec(memory_space=pltpu.VMEM)
    shape = jax.ShapeDtypeStruct((blocks, TILE), F32)
    return pl.pallas_call(
        functools.partial(fold_kernel, members, groups),
        out_shape=(shape, shape),
        in_specs=[vmem],
        out_specs=(vmem, vmem),
        scratch_shapes=[
            pltpu.VMEM((members, 2, blocks, TILE), F32),
            pltpu.VMEM((2, blocks, TILE), F32),
            pltpu.VMEM((groups, 2, blocks, TILE), F32),
            dma((members,)), dma((members,)), dma((groups,)), dma((groups,)),
        ],
        compiler_params=pltpu.CompilerParams(
            collective_id=2, has_side_effects=True, vmem_limit_bytes=40 * 1024 * 1024
        ),
        name="fold_everywhere",
    )(part)


def per_device(mesh, frames, medoids, tile_ids, tile_counts, plan):
    width = frames.shape[1]
    blocks = frames.shape[0] // TILE
    member = lax.axis_index("frames").astype(jnp.int32)
    members, copies = mesh.shape["frames"], mesh.shape["medoids"]
    longest = tile_ids.shape[2]
    tiles = frames.reshape(blocks, TILE, width)
    medoid_tiles = medoids[0].reshape(-1, TILE, width)
    norm = jnp.sum(jnp.square(frames.astype(F32)), axis=1).reshape(blocks, TILE)
    meta = jnp.concatenate([tile_ids[0], tile_counts[0][:, None]], axis=1)
    meta = jnp.pad(meta, ((0, 0), (0, LANES - longest - 1)))
    zero = jnp.int32(0)
    by_frames = (
        frames.shape[0] <= medoids.shape[1]
        and copies & (copies - 1) == 0
        and blocks % copies == 0
        and members > 1
    )
    if by_frames:
        base = jnp.stack([member * medoid_tiles.shape[0], zero])
        tiles, meta, norm = gather_frames(mesh, tiles, meta, norm)
    else:
        base = jnp.stack([zero, member * blocks])
        medoid_tiles = gather_medoids(mesh, medoid_tiles)
    part = pair_minima(base, meta, plan, tiles, norm, medoid_tiles, longest)
    first, second = fold_everywhere(mesh, part, blocks)
    return first.reshape(-1), second.reshape(-1)


def solution(mesh):
    placed = (
        P(("slab", "frames"), None),
        P("medoids", "frames", None),
        P("medoids", ("slab", "frames"), None),
        P("medoids", ("slab", "frames")),
        P("slab"),
    )
    return jax.shard_map(
        functools.partial(per_device, mesh),
        mesh=mesh,
        in_specs=placed,
        out_specs=(P(("slab", "frames")), P(("slab", "frames"))),
        check_vma=False,
    )
```

```python
import functools

import jax
import jax.numpy as jnp
from jax import lax
from jax.experimental import pallas as pl
from jax.experimental.pallas import tpu as pltpu
from jax.sharding import PartitionSpec as P

TILE = 128
BIG = 1e30
UNROLL = 4
LANES = 128
MESH = pl.DeviceIdType.MESH
F32 = jnp.float32


def remote(src, dst, send, recv, where):
    return pltpu.make_async_remote_copy(
        src_ref=src, dst_ref=dst, send_sem=send, recv_sem=recv, device_id=where, device_id_type=MESH
    )


def greet(targets):
    barrier = pltpu.get_barrier_semaphore()
    for where in targets:
        pl.semaphore_signal(barrier, inc=1, device_id=where, device_id_type=MESH)
    pl.semaphore_wait(barrier, len(targets))


def frame_gather_kernel(
    members, copies, parts, frames, meta, norm, all_frames, all_meta, all_norm,
    own_sem, meta_send, meta_recv, norm_send, norm_recv,
    right_send, left_send, chain_recv, swap_send, swap_recv,
):
    me = lax.axis_index("frames")
    rep = lax.axis_index("medoids")
    blocks = frames.shape[0]
    share = blocks // copies
    piece = share // parts
    levels = copies.bit_length() - 1

    partners = []
    for level in range(levels):
        bit = copies >> (level + 1)
        partners.append((bit, {"medoids": rep + bit - 2 * bit * lax.rem(rep // bit, 2)}))
    others = [{"frames": lax.rem(me + k, members)} for k in range(1, members)]
    greet(others + [p[1] for p in partners])

    def place(block, owner_rep, part):
        return pl.ds(block * blocks + owner_rep * share + part * piece, piece)

    def chain(block, part, src, sends, to):
        return remote(
            src, all_frames.at[place(block, rep, part)], sends.at[block, part],
            chain_recv.at[block, part], {"frames": to},
        )

    def own_part(part):
        return frames.at[pl.ds(rep * share + part * piece, piece)]

    def held_part(block, part):
        return all_frames.at[place(block, rep, part)]

    for part in range(parts):
        @pl.when(me < members - 1)
        def _():
            chain(me, part, own_part(part), right_send, me + 1).start()

        @pl.when(me > 0)
        def _():
            chain(me, part, own_part(part), left_send, me - 1).start()

    own = pltpu.make_async_copy(frames, all_frames.at[pl.ds(me * blocks, blocks)], own_sem.at[0])
    own.start()
    own_meta = pltpu.make_async_copy(meta, all_meta.at[me], own_sem.at[1])
    own_meta.start()
    own_norm = pltpu.make_async_copy(norm, all_norm.at[me], own_sem.at[2])
    own_norm.start()
    small = []
    for k, where in enumerate(others):
        small.append(remote(meta, all_meta.at[me], meta_send.at[k], meta_recv.at[k], where))
        small.append(remote(norm, all_norm.at[me], norm_send.at[k], norm_recv.at[k], where))
    for copy in small:
        copy.start()

    def swap(block, part, level, index):
        holder = rep
        for earlier in range(level):
            if (index >> earlier) & 1:
                bit = partners[earlier][0]
                holder = holder + bit - 2 * bit * lax.rem(rep // bit, 2)
        slot = (1 << level) - 1 + index
        ref = all_frames.at[place(block, holder, part)]
        return remote(
            ref, ref, swap_send.at[block, part, slot], swap_recv.at[block, part, slot],
            partners[level][1],
        )

    def sides(step):
        return ((me - step >= 0, me - step, 0), (me + step <= members - 1, me + step, 1))

    def at_arrival(step, part):
        for exists, block, side in sides(step):
            @pl.when(exists)
            def _():
                chain(block, part, held_part(block, part), right_send, me).wait_recv()
                if side == 0:
                    @pl.when(me < members - 1)
                    def _():
                        chain(block, part, held_part(block, part), right_send, me + 1).start()
                else:
                    @pl.when(me > 0)
                    def _():
                        chain(block, part, held_part(block, part), left_send, me - 1).start()
                for level in range(levels):
                    swap(block, part, level, 0).start()

    def at_level(step, part, level):
        for exists, block, _side in sides(step):
            @pl.when(exists)
            def _():
                for index in range(1 << level):
                    swap(block, part, level, index).wait_recv()
                    mine = index | (1 << level)
                    for later in range(level + 1, levels):
                        swap(block, part, later, mine).start()

    units = [(step, part) for step in range(1, members) for part in range(parts)]
    for unit in units:
        at_arrival(*unit)
    for level in range(levels):
        for unit in units:
            at_level(*unit, level)

    own.wait()
    own_meta.wait()
    own_norm.wait()
    for copy in small:
        copy.wait_send()
        copy.wait_recv()
    for part in range(parts):
        @pl.when(me < members - 1)
        def _():
            chain(me, part, own_part(part), right_send, me + 1).wait_send()

        @pl.when(me > 0)
        def _():
            chain(me, part, own_part(part), left_send, me - 1).wait_send()
    for step, part in units:
        for exists, block, side in sides(step):
            @pl.when(exists)
            def _():
                if side == 0:
                    @pl.when(me < members - 1)
                    def _():
                        chain(block, part, held_part(block, part), right_send, me + 1).wait_send()
                else:
                    @pl.when(me > 0)
                    def _():
                        chain(block, part, held_part(block, part), left_send, me - 1).wait_send()
                for level in range(levels):
                    for index in range(1 << level):
                        swap(block, part, level, index).wait_send()


def gather_frames(mesh, tiles, meta, norm):
    members, copies = mesh.shape["frames"], mesh.shape["medoids"]
    blocks = tiles.shape[0]
    share = blocks // copies
    parts = 2 if share % 2 == 0 else 1
    dma = pltpu.SemaphoreType.DMA
    hbm = pl.BlockSpec(memory_space=pl.ANY)
    slots = max(copies - 1, 1)
    all_tiles, all_meta, all_norm = pl.pallas_call(
        functools.partial(frame_gather_kernel, members, copies, parts),
        out_shape=(
            jax.ShapeDtypeStruct((members * blocks,) + tiles.shape[1:], tiles.dtype),
            jax.ShapeDtypeStruct((members,) + meta.shape, meta.dtype),
            jax.ShapeDtypeStruct((members,) + norm.shape, norm.dtype),
        ),
        in_specs=[hbm] * 3,
        out_specs=(hbm,) * 3,
        scratch_shapes=[
            dma((3,)), dma((members,)), dma((members,)), dma((members,)), dma((members,)),
            dma((members, parts)), dma((members, parts)), dma((members, parts)),
            dma((members, parts, slots)), dma((members, parts, slots)),
        ],
        compiler_params=pltpu.CompilerParams(collective_id=0, has_side_effects=True),
        name="gather_frames",
    )(tiles, meta, norm)
    return all_tiles, all_meta.reshape(-1, LANES), all_norm.reshape(-1, LANES)


def medoid_gather_kernel(members, part, whole, own_sem, send_sem, recv_sem):
    me = lax.axis_index("frames")
    count = part.shape[0]
    others = [{"frames": lax.rem(me + k, members)} for k in range(1, members)]
    if others:
        greet(others)
    mine = whole.at[pl.ds(me * count, count)]
    own = pltpu.make_async_copy(part, mine, own_sem)
    own.start()
    sent = [remote(part, mine, send_sem.at[k], recv_sem.at[k], w) for k, w in enumerate(others)]
    for copy in sent:
        copy.start()
    own.wait()
    for copy in sent:
        copy.wait_send()
        copy.wait_recv()


def gather_medoids(mesh, tiles):
    members = mesh.shape["frames"]
    dma = pltpu.SemaphoreType.DMA
    return pl.pallas_call(
        functools.partial(medoid_gather_kernel, members),
        out_shape=jax.ShapeDtypeStruct((members * tiles.shape[0],) + tiles.shape[1:], tiles.dtype),
        in_specs=[pl.BlockSpec(memory_space=pl.ANY)],
        out_specs=pl.BlockSpec(memory_space=pl.ANY),
        scratch_shapes=[dma, dma((members,)), dma((members,))],
        compiler_params=pltpu.CompilerParams(collective_id=1, has_side_effects=True),
        name="gather_medoids",
    )(tiles)


def fold_two(left_one, left_two, right_one, right_two):
    first = jnp.minimum(left_one, right_one)
    second = jnp.minimum(jnp.maximum(left_one, right_one), jnp.minimum(left_two, right_two))
    return first, second


def pairs_kernel(
    longest, base, meta, plan, frames, norm, medoids, out,
    queue_frame, queue_medoid, half_norm, best_one, best_two, final_one, final_two,
):
    number = frames.shape[0]
    held = medoids.shape[0]
    width = frames.shape[2]
    rows = 8
    medoid_base, frame_base = base[0], base[1]

    def half(index, carry):
        tile = medoids[index].astype(F32)
        total = jnp.sum(tile * tile, axis=1, keepdims=True) * 0.5
        half_norm[index] = jnp.broadcast_to(total, (TILE, TILE))
        return carry

    lax.fori_loop(0, held, half, 0)

    def list_of(index, at):
        def entry(place, at):
            medoid = meta[index, place] - medoid_base
            queue_frame[at] = index
            queue_medoid[at] = medoid
            inside = jnp.logical_and(medoid >= 0, medoid < held)
            return at + inside.astype(jnp.int32)

        return lax.fori_loop(0, meta[index, longest], entry, at)

    length = lax.fori_loop(0, number, list_of, jnp.int32(0))
    for k in range(UNROLL):
        queue_frame[length + k] = number
        queue_medoid[length + k] = 0

    best_one[...] = jnp.full(best_one.shape, BIG, F32)
    best_two[...] = jnp.full(best_two.shape, BIG, F32)

    def work(step, carry):
        found = []
        for k in range(UNROLL):
            at = step * UNROLL + k
            row = queue_frame[at]
            medoid = queue_medoid[at]
            frame = jnp.minimum(row, number - 1)
            inner = lax.dot_general(
                medoids[medoid], frames[frame], (((1,), (1,)), ((), ())),
                preferred_element_type=F32,
            )
            value = half_norm[medoid] - inner
            chains = []
            for start in range(0, TILE, 4 * rows):
                parts = [value[start + i * rows:start + (i + 1) * rows] for i in range(4)]
                a, b = jnp.minimum(parts[0], parts[1]), jnp.maximum(parts[0], parts[1])
                c, d = jnp.minimum(parts[2], parts[3]), jnp.maximum(parts[2], parts[3])
                chains.append(fold_two(a, b, c, d))
            while len(chains) > 1:
                chains = [fold_two(*chains[i], *chains[i + 1]) for i in range(0, len(chains), 2)]
            found.append((row, chains[0]))
        for row, (one, two) in found:
            best_one[row], best_two[row] = fold_two(best_one[row], best_two[row], one, two)
        return carry

    lax.fori_loop(0, (length + UNROLL - 1) // UNROLL, work, 0)

    one, two = best_one[:number, 0, :], best_two[:number, 0, :]
    for i in range(1, rows):
        one, two = fold_two(one, two, best_one[:number, i, :], best_two[:number, i, :])
    final_one[...] = (norm[...] + 2.0 * one) / width
    final_two[...] = (norm[...] + 2.0 * two) / width

    def arrange(position, carry):
        source = plan[position] - frame_base
        mine = jnp.logical_and(source >= 0, source < number)
        row = jnp.clip(source, 0, number - 1)
        out[0, pl.ds(position, 1), :] = jnp.where(mine, final_one[pl.ds(row, 1), :], BIG)
        out[1, pl.ds(position, 1), :] = jnp.where(mine, final_two[pl.ds(row, 1), :], BIG)
        return carry

    lax.fori_loop(0, plan.shape[0], arrange, 0)


def pair_minima(base, meta, plan, tiles, norm, medoid_tiles, longest):
    number, held = tiles.shape[0], medoid_tiles.shape[0]
    smem = pl.BlockSpec(memory_space=pltpu.SMEM)
    vmem = pl.BlockSpec(memory_space=pltpu.VMEM)
    room = number * longest + 2 * UNROLL
    return pl.pallas_call(
        functools.partial(pairs_kernel, longest),
        out_shape=jax.ShapeDtypeStruct((2, plan.shape[0], TILE), F32),
        in_specs=[smem, smem, smem, vmem, vmem, vmem],
        out_specs=vmem,
        scratch_shapes=[
            pltpu.SMEM((room,), jnp.int32),
            pltpu.SMEM((room,), jnp.int32),
            pltpu.VMEM((held, TILE, TILE), F32),
            pltpu.VMEM((number + 1, 8, TILE), F32),
            pltpu.VMEM((number + 1, 8, TILE), F32),
            pltpu.VMEM((number, TILE), F32),
            pltpu.VMEM((number, TILE), F32),
        ],
        compiler_params=pltpu.CompilerParams(vmem_limit_bytes=40 * 1024 * 1024),
        name="pair_minima",
    )(base, meta, plan, tiles, norm, medoid_tiles)


def fold_kernel(
    members, groups, part, first, second, from_members, joined, from_groups,
    send_one, recv_one, send_two, recv_two,
):
    me = lax.axis_index("frames")
    group = lax.axis_index("medoids")
    blocks = first.shape[0]
    ways = [lax.rem(me + k, members) for k in range(1, members)]
    greet(
        [{"frames": w} for w in ways]
        + [{"medoids": lax.rem(group + k, groups)} for k in range(1, groups)]
    )
    copies = []
    for k, way in enumerate(ways):
        rows = pl.ds(pl.multiple_of(way * blocks, blocks), blocks)
        copies.append(
            remote(part.at[:, rows, :], from_members.at[k], send_one.at[k], recv_one.at[k], {"frames": way})
        )
    for copy in copies:
        copy.start()
    mine = pl.ds(pl.multiple_of(me * blocks, blocks), blocks)
    one, two = part[0, mine, :], part[1, mine, :]
    for k, copy in enumerate(copies):
        copy.wait_recv()
        one, two = fold_two(one, two, from_members[k, 0], from_members[k, 1])
    joined[0] = one
    joined[1] = two
    across = []
    for k in range(groups - 1):
        across.append(
            remote(
                joined, from_groups.at[k], send_two.at[k], recv_two.at[k],
                {"medoids": lax.rem(group + k + 1, groups)},
            )
        )
    for copy in across:
        copy.start()
    for k, copy in enumerate(across):
        copy.wait_recv()
        one, two = fold_two(one, two, from_groups[k, 0], from_groups[k, 1])
    first[...] = one
    second[...] = two
    for copy in copies + across:
        copy.wait_send()


def fold_everywhere(mesh, part, blocks):
    members, groups = mesh.shape["frames"], mesh.shape["medoids"]
    dma = pltpu.SemaphoreType.DMA
    vmem = pl.BlockSpec(memory_space=pltpu.VMEM)
    shape = jax.ShapeDtypeStruct((blocks, TILE), F32)
    return pl.pallas_call(
        functools.partial(fold_kernel, members, groups),
        out_shape=(shape, shape),
        in_specs=[vmem],
        out_specs=(vmem, vmem),
        scratch_shapes=[
            pltpu.VMEM((members, 2, blocks, TILE), F32),
            pltpu.VMEM((2, blocks, TILE), F32),
            pltpu.VMEM((groups, 2, blocks, TILE), F32),
            dma((members,)), dma((members,)), dma((groups,)), dma((groups,)),
        ],
        compiler_params=pltpu.CompilerParams(
            collective_id=2, has_side_effects=True, vmem_limit_bytes=40 * 1024 * 1024
        ),
        name="fold_everywhere",
    )(part)


def per_device(mesh, frames, medoids, tile_ids, tile_counts, plan):
    width = frames.shape[1]
    blocks = frames.shape[0] // TILE
    member = lax.axis_index("frames").astype(jnp.int32)
    members, copies = mesh.shape["frames"], mesh.shape["medoids"]
    longest = tile_ids.shape[2]
    tiles = frames.reshape(blocks, TILE, width)
    medoid_tiles = medoids[0].reshape(-1, TILE, width)
    norm = jnp.sum(jnp.square(frames.astype(F32)), axis=1).reshape(blocks, TILE)
    meta = jnp.concatenate([tile_ids[0], tile_counts[0][:, None]], axis=1)
    meta = jnp.pad(meta, ((0, 0), (0, LANES - longest - 1)))
    zero = jnp.int32(0)
    by_frames = (
        frames.shape[0] <= medoids.shape[1]
        and copies & (copies - 1) == 0
        and blocks % copies == 0
        and members > 1
    )
    if by_frames:
        base = jnp.stack([member * medoid_tiles.shape[0], zero])
        tiles, meta, norm = gather_frames(mesh, tiles, meta, norm)
    else:
        base = jnp.stack([zero, member * blocks])
        medoid_tiles = gather_medoids(mesh, medoid_tiles)
    part = pair_minima(base, meta, plan, tiles, norm, medoid_tiles, longest)
    first, second = fold_everywhere(mesh, part, blocks)
    return first.reshape(-1), second.reshape(-1)


def solution(mesh):
    placed = (
        P(("slab", "frames"), None),
        P("medoids", "frames", None),
        P("medoids", ("slab", "frames"), None),
        P("medoids", ("slab", "frames")),
        P("slab"),
    )
    return jax.shard_map(
        functools.partial(per_device, mesh),
        mesh=mesh,
        in_specs=placed,
        out_specs=(P(("slab", "frames")), P(("slab", "frames"))),
        check_vma=False,
    )
```

```python
import functools

import jax
import jax.numpy as jnp
from jax import lax
from jax.experimental import pallas as pl
from jax.experimental.pallas import tpu as pltpu
from jax.sharding import PartitionSpec as P

TILE = 128
BIG = 1e30
UNROLL = 4
LANES = 128
MESH = pl.DeviceIdType.MESH
F32 = jnp.float32


def remote(src, dst, send, recv, where):
    return pltpu.make_async_remote_copy(
        src_ref=src, dst_ref=dst, send_sem=send, recv_sem=recv, device_id=where, device_id_type=MESH
    )


def greet(targets):
    barrier = pltpu.get_barrier_semaphore()
    for where in targets:
        pl.semaphore_signal(barrier, inc=1, device_id=where, device_id_type=MESH)
    pl.semaphore_wait(barrier, len(targets))


def frame_gather_kernel(
    members, copies, parts, frames, meta, norm, medoids, out, all_frames, all_meta, all_norm,
    half_norm, penalty, best_one, best_two, own_sem, meta_send, meta_recv, norm_send, norm_recv,
    right_send, left_send, chain_recv, swap_send, swap_recv,
):
    me = lax.axis_index("frames")
    rep = lax.axis_index("medoids")
    blocks = frames.shape[0]
    share = blocks // copies
    piece = share // parts
    levels = copies.bit_length() - 1

    partners = []
    for level in range(levels):
        bit = copies >> (level + 1)
        partners.append((bit, {"medoids": rep + bit - 2 * bit * lax.rem(rep // bit, 2)}))
    others = [{"frames": lax.rem(me + k, members)} for k in range(1, members)]
    greet(others + [p[1] for p in partners])

    def place(block, owner_rep, part):
        return pl.ds(block * blocks + owner_rep * share + part * piece, piece)

    def chain(block, part, src, sends, to):
        return remote(
            src, all_frames.at[place(block, rep, part)], sends.at[block, part],
            chain_recv.at[block, part], {"frames": to},
        )

    def own_part(part):
        return frames.at[pl.ds(rep * share + part * piece, piece)]

    def held_part(block, part):
        return all_frames.at[place(block, rep, part)]

    own = pltpu.make_async_copy(frames, all_frames.at[pl.ds(me * blocks, blocks)], own_sem.at[0])
    own.start()
    own_meta = pltpu.make_async_copy(meta, all_meta.at[me], own_sem.at[1])
    own_meta.start()
    own_norm = pltpu.make_async_copy(norm, all_norm.at[me], own_sem.at[2])
    own_norm.start()
    small = []
    for k, where in enumerate(others):
        small.append(remote(meta, all_meta.at[me], meta_send.at[k], meta_recv.at[k], where))
        small.append(remote(norm, all_norm.at[me], norm_send.at[k], norm_recv.at[k], where))
    for copy in small:
        copy.start()

    for part in range(parts):
        @pl.when(me < members - 1)
        def _():
            chain(me, part, own_part(part), right_send, me + 1).start()

        @pl.when(me > 0)
        def _():
            chain(me, part, own_part(part), left_send, me - 1).start()

    def swap(block, part, level, index):
        holder = rep
        for earlier in range(level):
            if (index >> earlier) & 1:
                bit = partners[earlier][0]
                holder = holder + bit - 2 * bit * lax.rem(rep // bit, 2)
        slot = (1 << level) - 1 + index
        ref = all_frames.at[place(block, holder, part)]
        return remote(
            ref, ref, swap_send.at[block, part, slot], swap_recv.at[block, part, slot],
            partners[level][1],
        )

    def sides(step):
        return ((me - step >= 0, me - step, 0), (me + step <= members - 1, me + step, 1))

    def at_arrival(step, part):
        for exists, block, side in sides(step):
            @pl.when(exists)
            def _():
                chain(block, part, held_part(block, part), right_send, me).wait_recv()
                if side == 0:
                    @pl.when(me < members - 1)
                    def _():
                        chain(block, part, held_part(block, part), right_send, me + 1).start()
                else:
                    @pl.when(me > 0)
                    def _():
                        chain(block, part, held_part(block, part), left_send, me - 1).start()
                for level in range(levels):
                    swap(block, part, level, 0).start()

    def at_level(step, part, level):
        for exists, block, _side in sides(step):
            @pl.when(exists)
            def _():
                for index in range(1 << level):
                    swap(block, part, level, index).wait_recv()
                    mine = index | (1 << level)
                    for later in range(level + 1, levels):
                        swap(block, part, later, mine).start()

    units = [(step, part) for step in range(1, members) for part in range(parts)]
    held = medoids.shape[0]
    width = medoids.shape[2]
    rows = 8
    wide = 2 if blocks % 2 == 0 else 1
    deep = 4 if held % 4 == 0 else 1

    def half(index, carry):
        tile = medoids[index].astype(F32)
        total = jnp.sum(tile * tile, axis=1, keepdims=True) * 0.5
        half_norm[index] = jnp.broadcast_to(total, (TILE, TILE))
        return carry

    lax.fori_loop(0, held, half, 0)
    own.wait()
    own_meta.wait()
    own_norm.wait()
    for copy in small:
        copy.wait_send()
        copy.wait_recv()

    def compute(block):
        def some(index, carry):
            at = block * blocks + index * wide
            for k in range(wide):
                row = all_meta[block, pl.ds(index * wide + k, 1), :]
                penalty[k] = jnp.broadcast_to(row, (LANES, LANES)).T
            batch = all_frames[pl.ds(at, wide)].reshape(wide * TILE, width)
            best = [None] * wide
            for start in range(0, held, deep):
                inner = lax.dot_general(
                    medoids[start:start + deep].reshape(deep * TILE, width), batch,
                    (((1,), (1,)), ((), ())), preferred_element_type=F32,
                )
                for j in range(deep):
                    for k in range(wide):
                        value = half_norm[start + j] - inner[
                            j * TILE:(j + 1) * TILE, k * TILE:(k + 1) * TILE
                        ]
                        found = fold_rows(value, rows)
                        more = penalty[k, pl.ds(me * held + start + j, 1), :]
                        found = (found[0] + more, found[1] + more)
                        best[k] = found if best[k] is None else fold_two(*best[k], *found)
            for k in range(wide):
                best_one[at + k] = best[k][0]
                best_two[at + k] = best[k][1]
            return carry

        lax.fori_loop(0, blocks // wide, some, 0)

    compute(me)

    def finish(step):
        for level in range(levels):
            for part in range(parts):
                at_level(step, part, level)
        for exists, block, _side in sides(step):
            @pl.when(exists)
            def _():
                compute(block)

    for step in range(1, members):
        for part in range(parts):
            at_arrival(step, part)
            if part == 0 and step > 1:
                finish(step - 1)
    finish(members - 1)

    total = all_norm[...].reshape(members * blocks, TILE)
    one, two = best_one[:, 0, :], best_two[:, 0, :]
    for i in range(1, rows):
        one, two = fold_two(one, two, best_one[:, i, :], best_two[:, i, :])
    out[0] = (total + 2.0 * one) / width
    out[1] = (total + 2.0 * two) / width

    for part in range(parts):
        @pl.when(me < members - 1)
        def _():
            chain(me, part, own_part(part), right_send, me + 1).wait_send()

        @pl.when(me > 0)
        def _():
            chain(me, part, own_part(part), left_send, me - 1).wait_send()
    for step, part in units:
        for exists, block, side in sides(step):
            @pl.when(exists)
            def _():
                if side == 0:
                    @pl.when(me < members - 1)
                    def _():
                        chain(block, part, held_part(block, part), right_send, me + 1).wait_send()
                else:
                    @pl.when(me > 0)
                    def _():
                        chain(block, part, held_part(block, part), left_send, me - 1).wait_send()
                for level in range(levels):
                    for index in range(1 << level):
                        swap(block, part, level, index).wait_send()


def gather_frames(mesh, tiles, meta, norm, medoid_tiles):
    members, copies = mesh.shape["frames"], mesh.shape["medoids"]
    blocks = tiles.shape[0]
    share = blocks // copies
    parts = 2 if share % 2 == 0 else 1
    dma = pltpu.SemaphoreType.DMA
    hbm = pl.BlockSpec(memory_space=pl.ANY)
    vmem = pl.BlockSpec(memory_space=pltpu.VMEM)
    slots = max(copies - 1, 1)
    number, held = members * blocks, medoid_tiles.shape[0]
    return pl.pallas_call(
        functools.partial(frame_gather_kernel, members, copies, parts),
        out_shape=jax.ShapeDtypeStruct((2, number, TILE), F32),
        in_specs=[hbm, vmem, vmem, vmem],
        out_specs=vmem,
        scratch_shapes=[
            pltpu.VMEM((number,) + tiles.shape[1:], tiles.dtype),
            pltpu.VMEM((members,) + meta.shape, meta.dtype),
            pltpu.VMEM((members,) + norm.shape, norm.dtype),
            pltpu.VMEM((held, TILE, TILE), F32),
            pltpu.VMEM((2, LANES, LANES), F32),
            pltpu.VMEM((number, 8, TILE), F32),
            pltpu.VMEM((number, 8, TILE), F32),
            dma((3,)), dma((members,)), dma((members,)), dma((members,)), dma((members,)),
            dma((members, parts)), dma((members, parts)), dma((members, parts)),
            dma((members, parts, slots)), dma((members, parts, slots)),
        ],
        compiler_params=pltpu.CompilerParams(
            collective_id=0, has_side_effects=True, vmem_limit_bytes=44 * 1024 * 1024
        ),
        name="gather_frames",
    )(tiles, meta, norm, medoid_tiles)


def arrange_kernel(plan, part, out):
    def one(position, carry):
        for k in range(2):
            out[k, pl.ds(position, 1), :] = part[k, pl.ds(plan[position], 1), :]
        return carry

    lax.fori_loop(0, plan.shape[0], one, 0)


def arrange(plan, part):
    vmem = pl.BlockSpec(memory_space=pltpu.VMEM)
    return pl.pallas_call(
        arrange_kernel,
        out_shape=jax.ShapeDtypeStruct(part.shape, F32),
        in_specs=[pl.BlockSpec(memory_space=pltpu.SMEM), vmem],
        out_specs=vmem,
        name="arrange",
    )(plan, part)


def medoid_gather_kernel(members, part, whole, own_sem, send_sem, recv_sem):
    me = lax.axis_index("frames")
    count = part.shape[0]
    others = [{"frames": lax.rem(me + k, members)} for k in range(1, members)]
    if others:
        greet(others)
    mine = whole.at[pl.ds(me * count, count)]
    own = pltpu.make_async_copy(part, mine, own_sem)
    own.start()
    sent = [remote(part, mine, send_sem.at[k], recv_sem.at[k], w) for k, w in enumerate(others)]
    for copy in sent:
        copy.start()
    own.wait()
    for copy in sent:
        copy.wait_send()
        copy.wait_recv()


def gather_medoids(mesh, tiles):
    members = mesh.shape["frames"]
    dma = pltpu.SemaphoreType.DMA
    return pl.pallas_call(
        functools.partial(medoid_gather_kernel, members),
        out_shape=jax.ShapeDtypeStruct((members * tiles.shape[0],) + tiles.shape[1:], tiles.dtype),
        in_specs=[pl.BlockSpec(memory_space=pl.ANY)],
        out_specs=pl.BlockSpec(memory_space=pl.ANY),
        scratch_shapes=[dma, dma((members,)), dma((members,))],
        compiler_params=pltpu.CompilerParams(collective_id=1, has_side_effects=True),
        name="gather_medoids",
    )(tiles)


def fold_two(left_one, left_two, right_one, right_two):
    first = jnp.minimum(left_one, right_one)
    second = jnp.minimum(jnp.maximum(left_one, right_one), jnp.minimum(left_two, right_two))
    return first, second


def fold_rows(value, rows):
    chains = []
    for start in range(0, TILE, 4 * rows):
        parts = [value[start + i * rows:start + (i + 1) * rows] for i in range(4)]
        a, b = jnp.minimum(parts[0], parts[1]), jnp.maximum(parts[0], parts[1])
        c, d = jnp.minimum(parts[2], parts[3]), jnp.maximum(parts[2], parts[3])
        chains.append(fold_two(a, b, c, d))
    while len(chains) > 1:
        chains = [fold_two(*chains[i], *chains[i + 1]) for i in range(0, len(chains), 2)]
    return chains[0]


def pairs_kernel(
    longest, base, meta, plan, frames, norm, medoids, out,
    queue_frame, queue_medoid, half_norm, best_one, best_two, final_one, final_two,
):
    number = frames.shape[0]
    held = medoids.shape[0]
    width = frames.shape[2]
    rows = 8
    medoid_base, frame_base = base[0], base[1]

    def half(index, carry):
        tile = medoids[index].astype(F32)
        total = jnp.sum(tile * tile, axis=1, keepdims=True) * 0.5
        half_norm[index] = jnp.broadcast_to(total, (TILE, TILE))
        return carry

    lax.fori_loop(0, held, half, 0)

    def list_of(index, at):
        def entry(place, at):
            medoid = meta[index, place] - medoid_base
            queue_frame[at] = index
            queue_medoid[at] = medoid
            inside = jnp.logical_and(medoid >= 0, medoid < held)
            return at + inside.astype(jnp.int32)

        return lax.fori_loop(0, meta[index, longest], entry, at)

    length = lax.fori_loop(0, number, list_of, jnp.int32(0))
    for k in range(UNROLL):
        queue_frame[length + k] = number
        queue_medoid[length + k] = 0

    best_one[...] = jnp.full(best_one.shape, BIG, F32)
    best_two[...] = jnp.full(best_two.shape, BIG, F32)

    def work(step, carry):
        found = []
        for k in range(UNROLL):
            at = step * UNROLL + k
            row = queue_frame[at]
            medoid = queue_medoid[at]
            frame = jnp.minimum(row, number - 1)
            inner = lax.dot_general(
                medoids[medoid], frames[frame], (((1,), (1,)), ((), ())),
                preferred_element_type=F32,
            )
            value = half_norm[medoid] - inner
            chains = []
            for start in range(0, TILE, 4 * rows):
                parts = [value[start + i * rows:start + (i + 1) * rows] for i in range(4)]
                a, b = jnp.minimum(parts[0], parts[1]), jnp.maximum(parts[0], parts[1])
                c, d = jnp.minimum(parts[2], parts[3]), jnp.maximum(parts[2], parts[3])
                chains.append(fold_two(a, b, c, d))
            while len(chains) > 1:
                chains = [fold_two(*chains[i], *chains[i + 1]) for i in range(0, len(chains), 2)]
            found.append((row, chains[0]))
        for row, (one, two) in found:
            best_one[row], best_two[row] = fold_two(best_one[row], best_two[row], one, two)
        return carry

    lax.fori_loop(0, (length + UNROLL - 1) // UNROLL, work, 0)

    one, two = best_one[:number, 0, :], best_two[:number, 0, :]
    for i in range(1, rows):
        one, two = fold_two(one, two, best_one[:number, i, :], best_two[:number, i, :])
    final_one[...] = (norm[...] + 2.0 * one) / width
    final_two[...] = (norm[...] + 2.0 * two) / width

    def arrange(position, carry):
        source = plan[position] - frame_base
        mine = jnp.logical_and(source >= 0, source < number)
        row = jnp.clip(source, 0, number - 1)
        out[0, pl.ds(position, 1), :] = jnp.where(mine, final_one[pl.ds(row, 1), :], BIG)
        out[1, pl.ds(position, 1), :] = jnp.where(mine, final_two[pl.ds(row, 1), :], BIG)
        return carry

    lax.fori_loop(0, plan.shape[0], arrange, 0)


def pair_minima(base, meta, plan, tiles, norm, medoid_tiles, longest):
    number, held = tiles.shape[0], medoid_tiles.shape[0]
    smem = pl.BlockSpec(memory_space=pltpu.SMEM)
    vmem = pl.BlockSpec(memory_space=pltpu.VMEM)
    room = number * longest + 2 * UNROLL
    return pl.pallas_call(
        functools.partial(pairs_kernel, longest),
        out_shape=jax.ShapeDtypeStruct((2, plan.shape[0], TILE), F32),
        in_specs=[smem, smem, smem, vmem, vmem, vmem],
        out_specs=vmem,
        scratch_shapes=[
            pltpu.SMEM((room,), jnp.int32),
            pltpu.SMEM((room,), jnp.int32),
            pltpu.VMEM((held, TILE, TILE), F32),
            pltpu.VMEM((number + 1, 8, TILE), F32),
            pltpu.VMEM((number + 1, 8, TILE), F32),
            pltpu.VMEM((number, TILE), F32),
            pltpu.VMEM((number, TILE), F32),
        ],
        compiler_params=pltpu.CompilerParams(vmem_limit_bytes=40 * 1024 * 1024),
        name="pair_minima",
    )(base, meta, plan, tiles, norm, medoid_tiles)


def fold_kernel(
    members, groups, part, first, second, from_members, joined, from_groups,
    send_one, recv_one, send_two, recv_two,
):
    me = lax.axis_index("frames")
    group = lax.axis_index("medoids")
    blocks = first.shape[0]
    ways = [lax.rem(me + k, members) for k in range(1, members)]
    greet(
        [{"frames": w} for w in ways]
        + [{"medoids": lax.rem(group + k, groups)} for k in range(1, groups)]
    )
    copies = []
    for k, way in enumerate(ways):
        rows = pl.ds(pl.multiple_of(way * blocks, blocks), blocks)
        copies.append(
            remote(part.at[:, rows, :], from_members.at[k], send_one.at[k], recv_one.at[k], {"frames": way})
        )
    for copy in copies:
        copy.start()
    mine = pl.ds(pl.multiple_of(me * blocks, blocks), blocks)
    one, two = part[0, mine, :], part[1, mine, :]
    for k, copy in enumerate(copies):
        copy.wait_recv()
        one, two = fold_two(one, two, from_members[k, 0], from_members[k, 1])
    joined[0] = one
    joined[1] = two
    across = []
    for k in range(groups - 1):
        across.append(
            remote(
                joined, from_groups.at[k], send_two.at[k], recv_two.at[k],
                {"medoids": lax.rem(group + k + 1, groups)},
            )
        )
    for copy in across:
        copy.start()
    for k, copy in enumerate(across):
        copy.wait_recv()
        one, two = fold_two(one, two, from_groups[k, 0], from_groups[k, 1])
    first[...] = one
    second[...] = two
    for copy in copies + across:
        copy.wait_send()


def fold_everywhere(mesh, part, blocks):
    members, groups = mesh.shape["frames"], mesh.shape["medoids"]
    dma = pltpu.SemaphoreType.DMA
    vmem = pl.BlockSpec(memory_space=pltpu.VMEM)
    shape = jax.ShapeDtypeStruct((blocks, TILE), F32)
    return pl.pallas_call(
        functools.partial(fold_kernel, members, groups),
        out_shape=(shape, shape),
        in_specs=[vmem],
        out_specs=(vmem, vmem),
        scratch_shapes=[
            pltpu.VMEM((members, 2, blocks, TILE), F32),
            pltpu.VMEM((2, blocks, TILE), F32),
            pltpu.VMEM((groups, 2, blocks, TILE), F32),
            dma((members,)), dma((members,)), dma((groups,)), dma((groups,)),
        ],
        compiler_params=pltpu.CompilerParams(
            collective_id=2, has_side_effects=True, vmem_limit_bytes=40 * 1024 * 1024
        ),
        name="fold_everywhere",
    )(part)


def per_device(mesh, frames, medoids, tile_ids, tile_counts, plan):
    width = frames.shape[1]
    blocks = frames.shape[0] // TILE
    member = lax.axis_index("frames").astype(jnp.int32)
    members, copies = mesh.shape["frames"], mesh.shape["medoids"]
    longest = tile_ids.shape[2]
    tiles = frames.reshape(blocks, TILE, width)
    medoid_tiles = medoids[0].reshape(-1, TILE, width)
    norm = jnp.sum(jnp.square(frames.astype(F32)), axis=1).reshape(blocks, TILE)
    by_frames = (
        frames.shape[0] <= medoids.shape[1]
        and copies & (copies - 1) == 0
        and blocks % copies == 0
        and members > 1
        and members * medoid_tiles.shape[0] <= LANES
    )
    if by_frames:
        live = jnp.arange(longest)[None, :] < tile_counts[0][:, None]
        same = tile_ids[0][:, :, None] == jnp.arange(LANES)[None, None, :]
        listed = jnp.any(jnp.logical_and(live[:, :, None], same), axis=1)
        barred = jnp.where(listed, 0.0, BIG).astype(F32)
        part = arrange(plan, gather_frames(mesh, tiles, barred, norm, medoid_tiles))
    else:
        meta = jnp.concatenate([tile_ids[0], tile_counts[0][:, None]], axis=1)
        meta = jnp.pad(meta, ((0, 0), (0, LANES - longest - 1)))
        base = jnp.stack([jnp.int32(0), member * blocks])
        medoid_tiles = gather_medoids(mesh, medoid_tiles)
        part = pair_minima(base, meta, plan, tiles, norm, medoid_tiles, longest)
    first, second = fold_everywhere(mesh, part, blocks)
    return first.reshape(-1), second.reshape(-1)


def solution(mesh):
    placed = (
        P(("slab", "frames"), None),
        P("medoids", "frames", None),
        P("medoids", ("slab", "frames"), None),
        P("medoids", ("slab", "frames")),
        P("slab"),
    )
    return jax.shard_map(
        functools.partial(per_device, mesh),
        mesh=mesh,
        in_specs=placed,
        out_specs=(P(("slab", "frames")), P(("slab", "frames"))),
        check_vma=False,
    )
```

```python
import functools

import jax
import jax.numpy as jnp
from jax import lax
from jax.experimental import pallas as pl
from jax.experimental.pallas import tpu as pltpu
from jax.sharding import PartitionSpec as P

TILE = 128
BIG = 1e30
UNROLL = 4
LANES = 128
MESH = pl.DeviceIdType.MESH
F32 = jnp.float32


def remote(src, dst, send, recv, where):
    return pltpu.make_async_remote_copy(
        src_ref=src, dst_ref=dst, send_sem=send, recv_sem=recv, device_id=where, device_id_type=MESH
    )


def greet(targets):
    barrier = pltpu.get_barrier_semaphore()
    for where in targets:
        pl.semaphore_signal(barrier, inc=1, device_id=where, device_id_type=MESH)
    pl.semaphore_wait(barrier, len(targets))


def frame_gather_kernel(
    members, copies, parts, frames, meta, medoids_far, out, all_frames, all_meta, all_norm,
    medoids, norm, half_norm, penalty, best_one, best_two, own_sem, meta_send, meta_recv, norm_send, norm_recv,
    right_send, left_send, chain_recv, swap_send, swap_recv,
):
    me = lax.axis_index("frames")
    rep = lax.axis_index("medoids")
    blocks = frames.shape[0]
    share = blocks // copies
    piece = share // parts
    levels = copies.bit_length() - 1

    partners = []
    for level in range(levels):
        bit = copies >> (level + 1)
        partners.append((bit, {"medoids": rep + bit - 2 * bit * lax.rem(rep // bit, 2)}))
    others = [{"frames": lax.rem(me + k, members)} for k in range(1, members)]
    greet(others + [p[1] for p in partners])

    def place(block, owner_rep, part):
        return pl.ds(block * blocks + owner_rep * share + part * piece, piece)

    def chain(block, part, src, sends, to):
        return remote(
            src, all_frames.at[place(block, rep, part)], sends.at[block, part],
            chain_recv.at[block, part], {"frames": to},
        )

    def own_part(part):
        return frames.at[pl.ds(rep * share + part * piece, piece)]

    def held_part(block, part):
        return all_frames.at[place(block, rep, part)]

    own = pltpu.make_async_copy(frames, all_frames.at[pl.ds(me * blocks, blocks)], own_sem.at[0])
    own.start()
    own_meta = pltpu.make_async_copy(meta, all_meta.at[me], own_sem.at[1])
    own_meta.start()
    fetch = pltpu.make_async_copy(medoids_far, medoids, own_sem.at[2])
    fetch.start()
    small = []
    norms = []
    for k, where in enumerate(others):
        small.append(remote(meta, all_meta.at[me], meta_send.at[k], meta_recv.at[k], where))
        norms.append(remote(norm, all_norm.at[me], norm_send.at[k], norm_recv.at[k], where))
    for copy in small:
        copy.start()

    for part in range(parts):
        @pl.when(me < members - 1)
        def _():
            chain(me, part, own_part(part), right_send, me + 1).start()

        @pl.when(me > 0)
        def _():
            chain(me, part, own_part(part), left_send, me - 1).start()

    def swap(block, part, level, index):
        holder = rep
        for earlier in range(level):
            if (index >> earlier) & 1:
                bit = partners[earlier][0]
                holder = holder + bit - 2 * bit * lax.rem(rep // bit, 2)
        slot = (1 << level) - 1 + index
        ref = all_frames.at[place(block, holder, part)]
        return remote(
            ref, ref, swap_send.at[block, part, slot], swap_recv.at[block, part, slot],
            partners[level][1],
        )

    def sides(step):
        return ((me - step >= 0, me - step, 0), (me + step <= members - 1, me + step, 1))

    def at_arrival(step, part):
        for exists, block, side in sides(step):
            @pl.when(exists)
            def _():
                chain(block, part, held_part(block, part), right_send, me).wait_recv()
                if side == 0:
                    @pl.when(me < members - 1)
                    def _():
                        chain(block, part, held_part(block, part), right_send, me + 1).start()
                else:
                    @pl.when(me > 0)
                    def _():
                        chain(block, part, held_part(block, part), left_send, me - 1).start()
                for level in range(levels):
                    swap(block, part, level, 0).start()

    def at_level(step, part, level):
        for exists, block, _side in sides(step):
            @pl.when(exists)
            def _():
                for index in range(1 << level):
                    swap(block, part, level, index).wait_recv()
                    mine = index | (1 << level)
                    for later in range(level + 1, levels):
                        swap(block, part, later, mine).start()

    units = [(step, part) for step in range(1, members) for part in range(parts)]
    held = medoids.shape[0]
    width = medoids.shape[2]
    rows = 8
    wide = 2 if blocks % 2 == 0 else 1
    deep = 4 if held % 4 == 0 else 1

    def half(index, carry):
        tile = medoids[index].astype(F32)
        total = jnp.sum(tile * tile, axis=1, keepdims=True) * 0.5
        half_norm[index] = jnp.broadcast_to(total, (TILE, TILE))
        return carry

    own.wait()
    for index in range(blocks):
        tile = all_frames[me * blocks + index].astype(F32)
        total = jnp.sum(tile * tile, axis=1, keepdims=True)
        norm[index:index + 1, :] = jnp.broadcast_to(total, (TILE, TILE)).T[:1]
    for copy in norms:
        copy.start()
    fetch.wait()
    lax.fori_loop(0, held, half, 0)
    own_meta.wait()
    for copy in small:
        copy.wait_send()
        copy.wait_recv()

    def compute(block):
        def some(index, carry):
            at = block * blocks + index * wide
            for k in range(wide):
                row = all_meta[block, pl.ds(index * wide + k, 1), :]
                penalty[k] = jnp.broadcast_to(row, (LANES, LANES)).T
            batch = all_frames[pl.ds(at, wide)].reshape(wide * TILE, width)
            best = [None] * wide
            for start in range(0, held, deep):
                inner = lax.dot_general(
                    medoids[start:start + deep].reshape(deep * TILE, width), batch,
                    (((1,), (1,)), ((), ())), preferred_element_type=F32,
                )
                for j in range(deep):
                    for k in range(wide):
                        value = half_norm[start + j] - inner[
                            j * TILE:(j + 1) * TILE, k * TILE:(k + 1) * TILE
                        ]
                        found = fold_rows(value, rows)
                        more = penalty[k, pl.ds(me * held + start + j, 1), :]
                        found = (found[0] + more, found[1] + more)
                        best[k] = found if best[k] is None else fold_two(*best[k], *found)
            for k in range(wide):
                best_one[at + k] = best[k][0]
                best_two[at + k] = best[k][1]
            return carry

        lax.fori_loop(0, blocks // wide, some, 0)

    compute(me)

    def finish(step):
        for level in range(levels):
            for part in range(parts):
                at_level(step, part, level)
        for exists, block, _side in sides(step):
            @pl.when(exists)
            def _():
                compute(block)

    for step in range(1, members):
        for part in range(parts):
            at_arrival(step, part)
            if part == 0 and step > 1:
                finish(step - 1)
    finish(members - 1)

    for copy in norms:
        copy.wait_send()
        copy.wait_recv()
    all_norm[me] = norm[...]
    total = all_norm[...].reshape(members * blocks, TILE)
    one, two = best_one[:, 0, :], best_two[:, 0, :]
    for i in range(1, rows):
        one, two = fold_two(one, two, best_one[:, i, :], best_two[:, i, :])
    out[0] = (total + 2.0 * one) / width
    out[1] = (total + 2.0 * two) / width

    for part in range(parts):
        @pl.when(me < members - 1)
        def _():
            chain(me, part, own_part(part), right_send, me + 1).wait_send()

        @pl.when(me > 0)
        def _():
            chain(me, part, own_part(part), left_send, me - 1).wait_send()
    for step, part in units:
        for exists, block, side in sides(step):
            @pl.when(exists)
            def _():
                if side == 0:
                    @pl.when(me < members - 1)
                    def _():
                        chain(block, part, held_part(block, part), right_send, me + 1).wait_send()
                else:
                    @pl.when(me > 0)
                    def _():
                        chain(block, part, held_part(block, part), left_send, me - 1).wait_send()
                for level in range(levels):
                    for index in range(1 << level):
                        swap(block, part, level, index).wait_send()


def gather_frames(mesh, tiles, meta, medoid_tiles):
    members, copies = mesh.shape["frames"], mesh.shape["medoids"]
    blocks = tiles.shape[0]
    share = blocks // copies
    parts = 2 if share % 2 == 0 else 1
    dma = pltpu.SemaphoreType.DMA
    hbm = pl.BlockSpec(memory_space=pl.ANY)
    vmem = pl.BlockSpec(memory_space=pltpu.VMEM)
    slots = max(copies - 1, 1)
    number, held = members * blocks, medoid_tiles.shape[0]
    return pl.pallas_call(
        functools.partial(frame_gather_kernel, members, copies, parts),
        out_shape=jax.ShapeDtypeStruct((2, number, TILE), F32),
        in_specs=[hbm, vmem, hbm],
        out_specs=vmem,
        scratch_shapes=[
            pltpu.VMEM((number,) + tiles.shape[1:], tiles.dtype),
            pltpu.VMEM((members,) + meta.shape, meta.dtype),
            pltpu.VMEM((members, blocks, TILE), F32),
            pltpu.VMEM(medoid_tiles.shape, medoid_tiles.dtype),
            pltpu.VMEM((blocks, TILE), F32),
            pltpu.VMEM((held, TILE, TILE), F32),
            pltpu.VMEM((2, LANES, LANES), F32),
            pltpu.VMEM((number, 8, TILE), F32),
            pltpu.VMEM((number, 8, TILE), F32),
            dma((3,)), dma((members,)), dma((members,)), dma((members,)), dma((members,)),
            dma((members, parts)), dma((members, parts)), dma((members, parts)),
            dma((members, parts, slots)), dma((members, parts, slots)),
        ],
        compiler_params=pltpu.CompilerParams(
            collective_id=0, has_side_effects=True, vmem_limit_bytes=44 * 1024 * 1024
        ),
        name="gather_frames",
    )(tiles, meta, medoid_tiles)


def arrange_kernel(plan, part, out):
    def one(position, carry):
        for k in range(2):
            out[k, pl.ds(position, 1), :] = part[k, pl.ds(plan[position], 1), :]
        return carry

    lax.fori_loop(0, plan.shape[0], one, 0)


def arrange(plan, part):
    vmem = pl.BlockSpec(memory_space=pltpu.VMEM)
    return pl.pallas_call(
        arrange_kernel,
        out_shape=jax.ShapeDtypeStruct(part.shape, F32),
        in_specs=[pl.BlockSpec(memory_space=pltpu.SMEM), vmem],
        out_specs=vmem,
        name="arrange",
    )(plan, part)


def medoid_gather_kernel(members, part, whole, own_sem, send_sem, recv_sem):
    me = lax.axis_index("frames")
    count = part.shape[0]
    others = [{"frames": lax.rem(me + k, members)} for k in range(1, members)]
    if others:
        greet(others)
    mine = whole.at[pl.ds(me * count, count)]
    own = pltpu.make_async_copy(part, mine, own_sem)
    own.start()
    sent = [remote(part, mine, send_sem.at[k], recv_sem.at[k], w) for k, w in enumerate(others)]
    for copy in sent:
        copy.start()
    own.wait()
    for copy in sent:
        copy.wait_send()
        copy.wait_recv()


def gather_medoids(mesh, tiles):
    members = mesh.shape["frames"]
    dma = pltpu.SemaphoreType.DMA
    return pl.pallas_call(
        functools.partial(medoid_gather_kernel, members),
        out_shape=jax.ShapeDtypeStruct((members * tiles.shape[0],) + tiles.shape[1:], tiles.dtype),
        in_specs=[pl.BlockSpec(memory_space=pl.ANY)],
        out_specs=pl.BlockSpec(memory_space=pl.ANY),
        scratch_shapes=[dma, dma((members,)), dma((members,))],
        compiler_params=pltpu.CompilerParams(collective_id=1, has_side_effects=True),
        name="gather_medoids",
    )(tiles)


def fold_two(left_one, left_two, right_one, right_two):
    first = jnp.minimum(left_one, right_one)
    second = jnp.minimum(jnp.maximum(left_one, right_one), jnp.minimum(left_two, right_two))
    return first, second


def fold_rows(value, rows):
    chains = []
    for start in range(0, TILE, 4 * rows):
        parts = [value[start + i * rows:start + (i + 1) * rows] for i in range(4)]
        a, b = jnp.minimum(parts[0], parts[1]), jnp.maximum(parts[0], parts[1])
        c, d = jnp.minimum(parts[2], parts[3]), jnp.maximum(parts[2], parts[3])
        chains.append(fold_two(a, b, c, d))
    while len(chains) > 1:
        chains = [fold_two(*chains[i], *chains[i + 1]) for i in range(0, len(chains), 2)]
    return chains[0]


def pairs_kernel(
    longest, base, meta, plan, frames, norm, medoids, out,
    queue_frame, queue_medoid, half_norm, best_one, best_two, final_one, final_two,
):
    number = frames.shape[0]
    held = medoids.shape[0]
    width = frames.shape[2]
    rows = 8
    medoid_base, frame_base = base[0], base[1]

    def half(index, carry):
        tile = medoids[index].astype(F32)
        total = jnp.sum(tile * tile, axis=1, keepdims=True) * 0.5
        half_norm[index] = jnp.broadcast_to(total, (TILE, TILE))
        return carry

    lax.fori_loop(0, held, half, 0)

    def list_of(index, at):
        def entry(place, at):
            medoid = meta[index, place] - medoid_base
            queue_frame[at] = index
            queue_medoid[at] = medoid
            inside = jnp.logical_and(medoid >= 0, medoid < held)
            return at + inside.astype(jnp.int32)

        return lax.fori_loop(0, meta[index, longest], entry, at)

    length = lax.fori_loop(0, number, list_of, jnp.int32(0))
    for k in range(UNROLL):
        queue_frame[length + k] = number
        queue_medoid[length + k] = 0

    best_one[...] = jnp.full(best_one.shape, BIG, F32)
    best_two[...] = jnp.full(best_two.shape, BIG, F32)

    def work(step, carry):
        found = []
        for k in range(UNROLL):
            at = step * UNROLL + k
            row = queue_frame[at]
            medoid = queue_medoid[at]
            frame = jnp.minimum(row, number - 1)
            inner = lax.dot_general(
                medoids[medoid], frames[frame], (((1,), (1,)), ((), ())),
                preferred_element_type=F32,
            )
            value = half_norm[medoid] - inner
            chains = []
            for start in range(0, TILE, 4 * rows):
                parts = [value[start + i * rows:start + (i + 1) * rows] for i in range(4)]
                a, b = jnp.minimum(parts[0], parts[1]), jnp.maximum(parts[0], parts[1])
                c, d = jnp.minimum(parts[2], parts[3]), jnp.maximum(parts[2], parts[3])
                chains.append(fold_two(a, b, c, d))
            while len(chains) > 1:
                chains = [fold_two(*chains[i], *chains[i + 1]) for i in range(0, len(chains), 2)]
            found.append((row, chains[0]))
        for row, (one, two) in found:
            best_one[row], best_two[row] = fold_two(best_one[row], best_two[row], one, two)
        return carry

    lax.fori_loop(0, (length + UNROLL - 1) // UNROLL, work, 0)

    one, two = best_one[:number, 0, :], best_two[:number, 0, :]
    for i in range(1, rows):
        one, two = fold_two(one, two, best_one[:number, i, :], best_two[:number, i, :])
    final_one[...] = (norm[...] + 2.0 * one) / width
    final_two[...] = (norm[...] + 2.0 * two) / width

    def arrange(position, carry):
        source = plan[position] - frame_base
        mine = jnp.logical_and(source >= 0, source < number)
        row = jnp.clip(source, 0, number - 1)
        out[0, pl.ds(position, 1), :] = jnp.where(mine, final_one[pl.ds(row, 1), :], BIG)
        out[1, pl.ds(position, 1), :] = jnp.where(mine, final_two[pl.ds(row, 1), :], BIG)
        return carry

    lax.fori_loop(0, plan.shape[0], arrange, 0)


def pair_minima(base, meta, plan, tiles, norm, medoid_tiles, longest):
    number, held = tiles.shape[0], medoid_tiles.shape[0]
    smem = pl.BlockSpec(memory_space=pltpu.SMEM)
    vmem = pl.BlockSpec(memory_space=pltpu.VMEM)
    room = number * longest + 2 * UNROLL
    return pl.pallas_call(
        functools.partial(pairs_kernel, longest),
        out_shape=jax.ShapeDtypeStruct((2, plan.shape[0], TILE), F32),
        in_specs=[smem, smem, smem, vmem, vmem, vmem],
        out_specs=vmem,
        scratch_shapes=[
            pltpu.SMEM((room,), jnp.int32),
            pltpu.SMEM((room,), jnp.int32),
            pltpu.VMEM((held, TILE, TILE), F32),
            pltpu.VMEM((number + 1, 8, TILE), F32),
            pltpu.VMEM((number + 1, 8, TILE), F32),
            pltpu.VMEM((number, TILE), F32),
            pltpu.VMEM((number, TILE), F32),
        ],
        compiler_params=pltpu.CompilerParams(vmem_limit_bytes=40 * 1024 * 1024),
        name="pair_minima",
    )(base, meta, plan, tiles, norm, medoid_tiles)


def fold_kernel(
    members, groups, part, first, second, from_members, joined, from_groups,
    send_one, recv_one, send_two, recv_two,
):
    me = lax.axis_index("frames")
    group = lax.axis_index("medoids")
    blocks = first.shape[0]
    ways = [lax.rem(me + k, members) for k in range(1, members)]
    greet(
        [{"frames": w} for w in ways]
        + [{"medoids": lax.rem(group + k, groups)} for k in range(1, groups)]
    )
    copies = []
    for k, way in enumerate(ways):
        rows = pl.ds(pl.multiple_of(way * blocks, blocks), blocks)
        copies.append(
            remote(part.at[:, rows, :], from_members.at[k], send_one.at[k], recv_one.at[k], {"frames": way})
        )
    for copy in copies:
        copy.start()
    mine = pl.ds(pl.multiple_of(me * blocks, blocks), blocks)
    one, two = part[0, mine, :], part[1, mine, :]
    for k, copy in enumerate(copies):
        copy.wait_recv()
        one, two = fold_two(one, two, from_members[k, 0], from_members[k, 1])
    joined[0] = one
    joined[1] = two
    across = []
    for k in range(groups - 1):
        across.append(
            remote(
                joined, from_groups.at[k], send_two.at[k], recv_two.at[k],
                {"medoids": lax.rem(group + k + 1, groups)},
            )
        )
    for copy in across:
        copy.start()
    for k, copy in enumerate(across):
        copy.wait_recv()
        one, two = fold_two(one, two, from_groups[k, 0], from_groups[k, 1])
    first[...] = one
    second[...] = two
    for copy in copies + across:
        copy.wait_send()


def fold_everywhere(mesh, part, blocks):
    members, groups = mesh.shape["frames"], mesh.shape["medoids"]
    dma = pltpu.SemaphoreType.DMA
    vmem = pl.BlockSpec(memory_space=pltpu.VMEM)
    shape = jax.ShapeDtypeStruct((blocks, TILE), F32)
    return pl.pallas_call(
        functools.partial(fold_kernel, members, groups),
        out_shape=(shape, shape),
        in_specs=[vmem],
        out_specs=(vmem, vmem),
        scratch_shapes=[
            pltpu.VMEM((members, 2, blocks, TILE), F32),
            pltpu.VMEM((2, blocks, TILE), F32),
            pltpu.VMEM((groups, 2, blocks, TILE), F32),
            dma((members,)), dma((members,)), dma((groups,)), dma((groups,)),
        ],
        compiler_params=pltpu.CompilerParams(
            collective_id=2, has_side_effects=True, vmem_limit_bytes=40 * 1024 * 1024
        ),
        name="fold_everywhere",
    )(part)


def per_device(mesh, frames, medoids, tile_ids, tile_counts, plan):
    width = frames.shape[1]
    blocks = frames.shape[0] // TILE
    member = lax.axis_index("frames").astype(jnp.int32)
    members, copies = mesh.shape["frames"], mesh.shape["medoids"]
    longest = tile_ids.shape[2]
    tiles = frames.reshape(blocks, TILE, width)
    medoid_tiles = medoids[0].reshape(-1, TILE, width)
    by_frames = (
        frames.shape[0] <= medoids.shape[1]
        and copies & (copies - 1) == 0
        and blocks % copies == 0
        and members > 1
        and members * medoid_tiles.shape[0] <= LANES
    )
    if by_frames:
        live = jnp.arange(longest)[None, :] < tile_counts[0][:, None]
        same = tile_ids[0][:, :, None] == jnp.arange(LANES)[None, None, :]
        listed = jnp.any(jnp.logical_and(live[:, :, None], same), axis=1)
        barred = jnp.where(listed, 0.0, BIG).astype(F32)
        part = arrange(plan, gather_frames(mesh, tiles, barred, medoid_tiles))
    else:
        meta = jnp.concatenate([tile_ids[0], tile_counts[0][:, None]], axis=1)
        meta = jnp.pad(meta, ((0, 0), (0, LANES - longest - 1)))
        base = jnp.stack([jnp.int32(0), member * blocks])
        norm = jnp.sum(jnp.square(frames.astype(F32)), axis=1).reshape(blocks, TILE)
        medoid_tiles = gather_medoids(mesh, medoid_tiles)
        part = pair_minima(base, meta, plan, tiles, norm, medoid_tiles, longest)
    first, second = fold_everywhere(mesh, part, blocks)
    return first.reshape(-1), second.reshape(-1)


def solution(mesh):
    placed = (
        P(("slab", "frames"), None),
        P("medoids", "frames", None),
        P("medoids", ("slab", "frames"), None),
        P("medoids", ("slab", "frames")),
        P("slab"),
    )
    return jax.shard_map(
        functools.partial(per_device, mesh),
        mesh=mesh,
        in_specs=placed,
        out_specs=(P(("slab", "frames")), P(("slab", "frames"))),
        check_vma=False,
    )
```
